32 devices in a mesh: expert: 32 (over z, y, x, core).
Axes of the slice: x: 2, y: 2, z: 4, core: 2. Of those that a mesh axis runs over, the one named last changes fastest.
Arguments:
- tokens: bfloat16 [2048, 3584], P('expert'), may hold values from -6 to 6
- expert_ids: int32 [2048, 8], P('expert'), may hold values from 0 to 31, all different within a row; in each aligned block of 64 rows (0 to 63, 64 to 127, ...) at most 24 rows name the same one
- gate_weights: float32 [2048, 8], P('expert'), may hold values from 0.05 to 1
- host: int32 [32], replicated, may hold values from 0 to 31, each once
- w_in: bfloat16 [32, 2, 3584, 2, 512], P('expert'), may hold values from -0.09375 to 0.09375
- w_out: bfloat16 [32, 2, 512, 3584], P('expert'), may hold values from -0.1875 to 0.1875
Outputs:
- moe_out: bfloat16 [2048, 3584], P('expert')
The draws below stay inside these ranges and needn't reach their ends.
Inputs may be any that keep to these rules, and one draw needn't show every extreme that they name: `expert_ids`: each row names 8 different experts; in the rows of one device no expert is named more than 24 times, a bound that some block reaches. A permutation: device d holds the weights of expert host[d].
All inputs are finite; a program needn't handle non-finite values.
Results may differ from the reference program's by a relative error of at most 0.011.
Values may be sent and summed in bfloat16 or wider, within the bound.
A program may use at most 192 MiB of HBM per device.

```python
import math
import jax
import jax.numpy as jnp
import numpy as np
from jax import lax

D = 3584
FFW = 1024
TOP = 8
TOK_DEV = 64
HALF = 512
EXPERTS = 32
MOST = 24
TOKENS = 2048
N_EXPERT = 32


def level_of(rng, dims, shards, low, largest):
    def one(dim, parts):
        steps = jax.random.uniform(jax.random.fold_in(jax.random.fold_in(rng, 6), dim), (parts,), jnp.float32, low / len(shards), largest / len(shards))
        return jnp.repeat(jnp.exp(steps), dims[dim] // parts).reshape((-1,) + (1,) * (len(dims) - dim - 1))

    loudness = one(*shards[0])
    for cut in shards[1:]:
        loudness = loudness * one(*cut)
    return loudness


def deal_out(own_key, own, number, rows, number_of, top, limit, slope):
    ranking = jax.random.permutation(own_key, number_of)
    packed, common = portions_of(number_of, rows * top, limit, slope, True), portions_of(number_of, rows * top, limit, slope, False)
    places = jnp.arange(number_of)

    def named(sizes, turn):
        used = int((sizes > 0).sum())
        fixed = max(1, used // 4)
        moved = fixed + (places - fixed + turn * (used - fixed)) % max(1, number_of - fixed)
        return jnp.zeros((number_of,), jnp.int32).at[ranking[jnp.where(places < fixed, places, moved)]].set(jnp.asarray(sizes, jnp.int32))

    sizes = jnp.where(number % 4 == 0, named(packed, number // 4), named(common, number - number // 4 - 1))
    mixed = jax.random.permutation(jax.random.fold_in(own, 3), number_of)
    giver, sink = mixed[0:number_of // 2 * 2:2], mixed[1:number_of // 2 * 2:2]
    room = jnp.minimum(sizes[giver] - 1, limit - sizes[sink]) // 2
    room = jnp.where((giver == ranking[0]) | (sink == ranking[0]) | (sizes[sink] == 0), 0, jnp.maximum(room, 0))
    moved = jax.random.randint(jax.random.fold_in(own, 4), (number_of // 2,), 0, 1 << 20) % (room + 1)
    sizes = sizes.at[giver].add(-moved).at[sink].add(moved)
    items = jnp.searchsorted(jnp.cumsum(sizes), jnp.arange(rows * top), side="right").astype(jnp.int32)
    grid = items.reshape(top, rows).T
    grid = grid[jax.random.permutation(jax.random.fold_in(own, 1), rows)]
    turn = jax.random.randint(jax.random.fold_in(own, 2), (rows, 1), 0, top)
    return jnp.take_along_axis(grid, (jnp.arange(top)[None, :] + turn) % top, axis=1)


def portions_of(count, total, reach, lean, full):
    portions = [(1 << 20) // math.isqrt(grade ** lean) + 1 for grade in range(1, count + 1)]
    largest = reach if full else min(reach, max(-(-total // count), total * portions[0] // sum(portions)))
    least = 1 if total - largest >= count - 1 else 0
    counts, surplus = [largest] + [least] * (count - 1), total - largest - least * (count - 1)
    while surplus > 0:
        candidates = [i for i in range(1, count) if counts[i] < largest] or [i for i in range(1, count) if counts[i] < reach]
        mass, left = sum([portions[i] for i in candidates]), surplus
        for i in candidates:
            addition = min(reach - counts[i], max(1, left * portions[i] // mass), surplus)
            counts[i] = counts[i] + addition
            surplus = surplus - addition
    return np.array(counts)


def normal_values(stream_key, dims, spread, reach, cuts=(), kind=jnp.bfloat16):
    array = jax.random.normal(stream_key, dims, jnp.float32) * spread
    if len(cuts) > 0:
        array = level_of(stream_key, dims, cuts, -0.22, 0.18) * array
    return jnp.clip(array, min=-reach, max=reach).astype(kind)


def setup_inputs(seed: int = 0) -> dict:
    streams_of = jax.random.split(jax.random.key(seed), 7)
    tokens = normal_values(streams_of[0], (TOKENS, D), 1.0, 6.0, ((0, 32),))
    expert_ids_keys = jax.random.split(jax.random.fold_in(streams_of[1], 1), TOKENS // TOK_DEV)
    expert_ids_turns = jax.random.permutation(jax.random.fold_in(streams_of[1], 3), TOKENS // TOK_DEV)
    expert_ids = jax.vmap(lambda own, number: deal_out(jax.random.fold_in(streams_of[1], 2), own, number, TOK_DEV, EXPERTS, TOP, MOST, 2))(expert_ids_keys, expert_ids_turns).reshape((TOKENS, TOP))
    gate_weights = jnp.clip(jnp.exp(math.log(1.0) - 2.9957323 * jax.random.uniform(streams_of[2], (TOKENS, TOP), jnp.float32) ** level_of(streams_of[2], (TOKENS, TOP), ((0, 32),), -0.2, 0.2)), 0.05, 1.0)
    host = jax.random.permutation(streams_of[3], EXPERTS).astype(jnp.int32)
    w_in = normal_values(streams_of[4], (EXPERTS, 2, D, 2, HALF), D ** -0.5, 0.09375, ((0, 32),))
    w_out = normal_values(streams_of[5], (EXPERTS, 2, HALF, D), FFW ** -0.5, 0.1875, ((0, 32),))
    return {"tokens": tokens, "expert_ids": expert_ids, "gate_weights": gate_weights, "host": host, "w_in": w_in, "w_out": w_out}


def reference(tokens, expert_ids, gate_weights, host, w_in, w_out):
    capacity = N_EXPERT * MOST
    flat_experts = expert_ids.reshape(-1).astype(jnp.int32)
    flat_gates = gate_weights.reshape(-1)
    total = flat_experts.shape[0]
    assignment = jnp.arange(total, dtype=jnp.int32)
    source = assignment // (TOK_DEV * TOP)
    onehot = (flat_experts[:, None] == jnp.arange(EXPERTS, dtype=jnp.int32)[None, :]).astype(jnp.int32)
    running = jnp.cumsum(onehot.reshape(N_EXPERT, TOK_DEV * TOP, EXPERTS), axis=1).reshape(total, EXPERTS)
    within = jnp.sum(running * onehot, axis=1) - 1
    slot = source * MOST + within
    table = jnp.full((EXPERTS, capacity), total, jnp.int32).at[flat_experts, slot].set(assignment)

    def one_expert(result, items):
        expert, first, second = items
        chosen = table[expert]
        valid = chosen < total
        safe = jnp.minimum(chosen, total - 1)
        token_rows = safe // TOP
        inputs = tokens[token_rows].astype(jnp.float32)
        projected = jnp.einsum("rd,hdgu->rhgu", inputs, first.astype(jnp.float32))
        hidden = (jax.nn.silu(projected[:, :, 0]) * projected[:, :, 1]).astype(jnp.bfloat16)
        output = jnp.einsum("rhu,hud->rd", hidden.astype(jnp.float32), second.astype(jnp.float32))
        output = output.astype(jnp.bfloat16).astype(jnp.float32)
        weight = jnp.where(valid, flat_gates[safe], jnp.float32(0.0))
        return result.at[token_rows].add(weight[:, None] * output), None

    start = jnp.zeros((tokens.shape[0], tokens.shape[1]), jnp.float32)
    result, _ = lax.scan(one_expert, start, (host.astype(jnp.int32), w_in, w_out))
    return result.astype(jnp.bfloat16)
```

```python
import functools

import jax
import jax.numpy as jnp
from jax import lax
from jax.experimental import pallas as pl
from jax.experimental.pallas import tpu as pltpu
from jax.sharding import PartitionSpec as P


def ffn_kernel(groups, blocks, group_rows, tile, place_ref, gate_ref, tok_ref, first_ref, second_ref,
               out_ref, rows, weight, hidden, result):
    step = pl.program_id(0)
    group_tokens = tok_ref.shape[0]
    block_rows = rows.shape[0] // blocks

    def selection(group):
        place = place_ref[pl.ds(group, 1), :]
        slots = lax.broadcasted_iota(jnp.int32, (group_rows, group_tokens), 0)
        return slots == place

    @pl.when(step < groups)
    def _():
        chosen = selection(step)
        begin = pl.multiple_of(step * group_rows, group_rows)
        here = pl.ds(begin, group_rows)
        gates = gate_ref[pl.ds(step, 1), :]
        weight[here, :] = jnp.sum(jnp.where(chosen, gates, 0.0), axis=1, keepdims=True)
        rows[here, :] = jnp.dot(
            chosen.astype(jnp.bfloat16), tok_ref[...], preferred_element_type=jnp.float32
        ).astype(jnp.bfloat16)

    @pl.when((step >= groups) & (step < groups + blocks))
    def _():
        begin = pl.multiple_of((step - groups) * block_rows, block_rows)
        here = pl.ds(begin, block_rows)
        halves, _, twice = first_ref.shape
        half = twice // 2
        per = half // tile

        @pl.loop(0, halves * per)
        def _(number):
            h, j = number // per, number % per
            at = pl.multiple_of(j * tile, tile)
            x = rows[here, :]
            g = jnp.dot(x, first_ref[h, :, pl.ds(at, tile)], preferred_element_type=jnp.float32)
            u = jnp.dot(x, first_ref[h, :, pl.ds(half + at, tile)], preferred_element_type=jnp.float32)
            value = g / (1.0 + jnp.exp(-g)) * u
            hidden[:, pl.ds(pl.multiple_of(number * tile, tile), tile)] = value.astype(jnp.bfloat16)

        @pl.loop(0, second_ref.shape[1] // tile)
        def _(number):
            at = pl.ds(pl.multiple_of(number * tile, tile), tile)
            y = jnp.dot(hidden[...], second_ref[:, at], preferred_element_type=jnp.float32)
            result[here, at] = (y * weight[here, :]).astype(jnp.bfloat16)

    @pl.when(step >= groups + blocks)
    def _():
        group = step - groups - blocks
        chosen = selection(group).astype(jnp.bfloat16)
        begin = pl.multiple_of(group * group_rows, group_rows)
        out_ref[...] = lax.dot_general(
            chosen, result[pl.ds(begin, group_rows), :], (((0,), (0,)), ((), ())),
            preferred_element_type=jnp.float32,
        ).astype(jnp.bfloat16)


def local(tokens, expert_ids, gate_weights, host, w_in, w_out):
    experts = lax.axis_size("expert")
    tok_dev, top_count = expert_ids.shape
    d_model = tokens.shape[1]
    slot_count = max(
        2, min(tok_dev // 2, (3 * tok_dev * top_count + 2 * experts - 1) // (2 * experts))
    )
    together = 4 if slot_count >= 16 else 8
    groups = experts // together
    group_rows = together * slot_count
    group_tokens = together * tok_dev
    blocks = 2
    total = groups * group_rows
    mine = host[lax.axis_index("expert")]

    routing = jnp.concatenate([expert_ids.astype(jnp.float32), gate_weights], axis=1)
    routing = lax.all_gather(routing, "expert", axis=0, tiled=True)
    everyone = lax.all_gather(tokens, "expert", axis=0, tiled=True)

    hit = routing[:, :top_count] == mine.astype(jnp.float32)
    gate = jnp.sum(jnp.where(hit, routing[:, top_count:], 0.0), axis=1).reshape(groups, group_tokens)
    named = jnp.any(hit, axis=1).reshape(experts, tok_dev)
    earlier = jnp.arange(tok_dev)[:, None] < jnp.arange(tok_dev)[None, :]
    rank = jnp.dot(
        named.astype(jnp.float32), earlier.astype(jnp.float32), preferred_element_type=jnp.float32
    ).astype(jnp.int32)
    source = jnp.arange(experts, dtype=jnp.int32)[:, None] % together
    place = jnp.where(named, source * slot_count + rank, -1).reshape(groups, group_tokens)

    halves, _, _, half = w_in.shape[1:]
    first = w_in[0].reshape(halves, d_model, 2 * half)
    second = w_out[0].reshape(halves * half, d_model)
    whole = lambda shape: pl.BlockSpec(shape, lambda i: (0,) * len(shape), pipeline_mode=pl.Buffered(1))
    partial = pl.pallas_call(
        functools.partial(ffn_kernel, groups, blocks, group_rows, 256),
        grid=(2 * groups + blocks,),
        out_shape=jax.ShapeDtypeStruct((experts * tok_dev, d_model), jnp.bfloat16),
        in_specs=[
            whole(place.shape),
            whole(gate.shape),
            pl.BlockSpec((group_tokens, d_model), lambda i: (jnp.minimum(i, groups - 1), 0)),
            whole(first.shape),
            whole(second.shape),
        ],
        out_specs=pl.BlockSpec((group_tokens, d_model), lambda i: (jnp.maximum(i - groups - blocks, 0), 0)),
        scratch_shapes=[
            pltpu.VMEM((total, d_model), jnp.bfloat16),
            pltpu.VMEM((total, 1), jnp.float32),
            pltpu.VMEM((total // blocks, halves * half), jnp.bfloat16),
            pltpu.VMEM((total, d_model), jnp.bfloat16),
        ],
        compiler_params=pltpu.CompilerParams(vmem_limit_bytes=60 * 1024 * 1024),
        cost_estimate=pl.CostEstimate(flops=17 * 10**9, bytes_accessed=52 * 10**6, transcendentals=10**6),
    )(place, gate, everyone, first, second)
    return lax.psum_scatter(partial, "expert", scatter_dimension=0, tiled=True)


def solution(mesh):
    in_specs = (
        P("expert", None),
        P("expert", None),
        P("expert", None),
        P(),
        P("expert", None, None, None, None),
        P("expert", None, None, None),
    )
    out_specs = P("expert", None)
    return jax.shard_map(local, mesh=mesh, in_specs=in_specs, out_specs=out_specs, check_vma=False)
```

```python
import functools

import jax
import jax.numpy as jnp
from jax import lax
from jax.experimental import pallas as pl
from jax.experimental.pallas import tpu as pltpu
from jax.sharding import PartitionSpec as P


def ffn_kernel(groups, blocks, group_rows, tile, place_ref, gate_ref, tok_ref, first_ref, second_ref,
               out_ref, rows, weight, hidden, result):
    step = pl.program_id(0)
    group_tokens = tok_ref.shape[0]
    block_rows = rows.shape[0] // blocks

    def selection(group):
        place = place_ref[pl.ds(group, 1), :]
        slots = lax.broadcasted_iota(jnp.int32, (group_rows, group_tokens), 0)
        return slots == place

    @pl.when(step < groups)
    def _():
        chosen = selection(step)
        begin = pl.multiple_of(step * group_rows, group_rows)
        here = pl.ds(begin, group_rows)
        gates = gate_ref[pl.ds(step, 1), :]
        weight[here, :] = jnp.sum(jnp.where(chosen, gates, 0.0), axis=1, keepdims=True)
        rows[here, :] = jnp.dot(
            chosen.astype(jnp.bfloat16), tok_ref[...], preferred_element_type=jnp.float32
        ).astype(jnp.bfloat16)

    @pl.when((step >= groups) & (step < groups + blocks))
    def _():
        begin = pl.multiple_of((step - groups) * block_rows, block_rows)
        here = pl.ds(begin, block_rows)
        halves, _, twice = first_ref.shape
        half = twice // 2
        per = half // tile

        @pl.loop(0, halves * per)
        def _(number):
            h, j = number // per, number % per
            at = pl.multiple_of(j * tile, tile)
            x = rows[here, :]
            g = jnp.dot(x, first_ref[h, :, pl.ds(at, tile)], preferred_element_type=jnp.float32)
            u = jnp.dot(x, first_ref[h, :, pl.ds(half + at, tile)], preferred_element_type=jnp.float32)
            value = g / (1.0 + jnp.exp(-g)) * u
            hidden[:, pl.ds(pl.multiple_of(number * tile, tile), tile)] = value.astype(jnp.bfloat16)

        @pl.loop(0, second_ref.shape[1] // tile)
        def _(number):
            at = pl.ds(pl.multiple_of(number * tile, tile), tile)
            y = jnp.dot(hidden[...], second_ref[:, at], preferred_element_type=jnp.float32)
            result[here, at] = (y * weight[here, :]).astype(jnp.bfloat16)

    @pl.when(step >= groups + blocks)
    def _():
        group = step - groups - blocks
        chosen = selection(group).astype(jnp.bfloat16)
        begin = pl.multiple_of(group * group_rows, group_rows)
        out_ref[...] = lax.dot_general(
            chosen, result[pl.ds(begin, group_rows), :], (((0,), (0,)), ((), ())),
            preferred_element_type=jnp.float32,
        ).astype(jnp.bfloat16)


def local(tokens, expert_ids, gate_weights, host, w_in, w_out):
    experts = lax.axis_size("expert")
    tok_dev, top_count = expert_ids.shape
    d_model = tokens.shape[1]
    slot_count = max(
        2, min(tok_dev // 2, (3 * tok_dev * top_count + 2 * experts - 1) // (2 * experts))
    )
    sources = experts // 2
    together = 4 if slot_count >= 16 else 8
    groups = sources // together
    group_rows = together * slot_count
    group_tokens = together * tok_dev
    total = groups * group_rows
    mine = host[lax.axis_index("expert")]
    same_core = [list(range(core, experts, 2)) for core in range(2)]
    sibling = [(device, device ^ 1) for device in range(experts)]

    high = lax.reduce_precision(gate_weights, 8, 7)
    middle = lax.reduce_precision(gate_weights - high, 8, 7)
    low = gate_weights - high - middle
    routing = jnp.concatenate([expert_ids.astype(jnp.float32), high, middle, low], axis=1)
    routing = jnp.pad(routing, ((0, 0), (0, 128 - 4 * top_count)))
    outgoing = jnp.concatenate([tokens, routing.astype(jnp.bfloat16)], axis=1)
    own = lax.all_gather(outgoing, "expert", axis=0, tiled=True, axis_index_groups=same_core)
    other = lax.ppermute(own, "expert", sibling)

    halves, _, _, half = w_in.shape[1:]
    first = w_in[0].reshape(halves, d_model, 2 * half)
    second = w_out[0].reshape(halves * half, d_model)

    def partial_rows(gathered):
        routing = gathered[:, d_model:].astype(jnp.float32)
        ids, high, middle, low = (
            routing[:, part * top_count:(part + 1) * top_count] for part in range(4)
        )
        hit = ids == mine.astype(jnp.float32)
        gate = jnp.sum(jnp.where(hit, high + middle + low, 0.0), axis=1).reshape(groups, group_tokens)
        named = jnp.any(hit, axis=1).reshape(sources, tok_dev)
        earlier = jnp.arange(tok_dev)[:, None] < jnp.arange(tok_dev)[None, :]
        rank = jnp.dot(
            named.astype(jnp.float32), earlier.astype(jnp.float32), preferred_element_type=jnp.float32
        ).astype(jnp.int32)
        source = jnp.arange(sources, dtype=jnp.int32)[:, None] % together
        place = jnp.where(named, source * slot_count + rank, -1).reshape(groups, group_tokens)
        whole = lambda shape: pl.BlockSpec(
            shape, lambda i: (0,) * len(shape), pipeline_mode=pl.Buffered(1)
        )
        return pl.pallas_call(
            functools.partial(ffn_kernel, groups, 1, group_rows, 256),
            grid=(2 * groups + 1,),
            out_shape=jax.ShapeDtypeStruct((sources * tok_dev, d_model), jnp.bfloat16),
            in_specs=[
                whole(place.shape),
                whole(gate.shape),
                pl.BlockSpec((group_tokens, d_model), lambda i: (jnp.minimum(i, groups - 1), 0)),
                whole(first.shape),
                whole(second.shape),
            ],
            out_specs=pl.BlockSpec(
                (group_tokens, d_model), lambda i: (jnp.maximum(i - groups - 1, 0), 0)
            ),
            scratch_shapes=[
                pltpu.VMEM((total, d_model), jnp.bfloat16),
                pltpu.VMEM((total, 1), jnp.float32),
                pltpu.VMEM((total, halves * half), jnp.bfloat16),
                pltpu.VMEM((total, d_model), jnp.bfloat16),
            ],
            compiler_params=pltpu.CompilerParams(vmem_limit_bytes=56 * 1024 * 1024),
            cost_estimate=pl.CostEstimate(
                flops=17 * 10**9, bytes_accessed=40 * 10**6, transcendentals=10**6
            ),
        )(place, gate, gathered, first, second)

    kept = partial_rows(own)
    handed = lax.ppermute(partial_rows(other), "expert", sibling)
    summed = (kept.astype(jnp.float32) + handed.astype(jnp.float32)).astype(jnp.bfloat16)
    return lax.psum_scatter(
        summed, "expert", scatter_dimension=0, tiled=True, axis_index_groups=same_core
    )


def solution(mesh):
    in_specs = (
        P("expert", None),
        P("expert", None),
        P("expert", None),
        P(),
        P("expert", None, None, None, None),
        P("expert", None, None, None),
    )
    out_specs = P("expert", None)
    return jax.shard_map(local, mesh=mesh, in_specs=in_specs, out_specs=out_specs, check_vma=False)
```

```python
import functools

import jax
import jax.numpy as jnp
from jax import lax
from jax.experimental import pallas as pl
from jax.experimental.pallas import tpu as pltpu
from jax.sharding import PartitionSpec as P


def ffn_kernel(groups, blocks, group_rows, tile, place_ref, gate_ref, tok_ref, first_ref, second_ref,
               out_ref, rows, weight, hidden, result):
    step = pl.program_id(0)
    group_tokens = tok_ref.shape[0]
    block_rows = rows.shape[0] // blocks

    def selection(group):
        place = place_ref[pl.ds(group, 1), :]
        slots = lax.broadcasted_iota(jnp.int32, (group_rows, group_tokens), 0)
        return slots == place

    @pl.when(step < groups)
    def _():
        chosen = selection(step)
        begin = pl.multiple_of(step * group_rows, group_rows)
        here = pl.ds(begin, group_rows)
        gates = gate_ref[pl.ds(step, 1), :]
        weight[here, :] = jnp.sum(jnp.where(chosen, gates, 0.0), axis=1, keepdims=True)
        rows[here, :] = jnp.dot(
            chosen.astype(jnp.bfloat16), tok_ref[...], preferred_element_type=jnp.float32
        ).astype(jnp.bfloat16)

    @pl.when((step >= groups) & (step < groups + blocks))
    def _():
        begin = pl.multiple_of((step - groups) * block_rows, block_rows)
        here = pl.ds(begin, block_rows)
        halves, _, twice = first_ref.shape
        half = twice // 2
        per = half // tile

        @pl.loop(0, halves * per)
        def _(number):
            h, j = number // per, number % per
            at = pl.multiple_of(j * tile, tile)
            x = rows[here, :]
            g = jnp.dot(x, first_ref[h, :, pl.ds(at, tile)], preferred_element_type=jnp.float32)
            u = jnp.dot(x, first_ref[h, :, pl.ds(half + at, tile)], preferred_element_type=jnp.float32)
            value = g / (1.0 + jnp.exp(-g)) * u
            hidden[:, pl.ds(pl.multiple_of(number * tile, tile), tile)] = value.astype(jnp.bfloat16)

        @pl.loop(0, second_ref.shape[1] // tile)
        def _(number):
            at = pl.ds(pl.multiple_of(number * tile, tile), tile)
            y = jnp.dot(hidden[...], second_ref[:, at], preferred_element_type=jnp.float32)
            result[here, at] = (y * weight[here, :]).astype(jnp.bfloat16)

    @pl.when(step >= groups + blocks)
    def _():
        group = step - groups - blocks
        chosen = selection(group).astype(jnp.bfloat16)
        begin = pl.multiple_of(group * group_rows, group_rows)
        out_ref[...] = lax.dot_general(
            chosen, result[pl.ds(begin, group_rows), :], (((0,), (0,)), ((), ())),
            preferred_element_type=jnp.float32,
        ).astype(jnp.bfloat16)


def exchange_orders(experts):
    bits = experts.bit_length() - 1
    middle = list(range(1, bits - 1))
    return [middle[k % len(middle):] + middle[:k % len(middle)] + [bits - 1] for k in range(3)]


def column_parts(width):
    tiles = width // 128
    cuts = [tiles * k // 3 * 128 for k in range(3)] + [width]
    return list(zip(cuts[:-1], cuts[1:]))


def swap(block, bit, experts):
    return lax.ppermute(block, "expert", [(i, i ^ (1 << bit)) for i in range(experts)])


def gather_chips(block, experts):
    parts = [block[:, low:high] for low, high in column_parts(block.shape[1])]
    orders = [order[::-1] for order in exchange_orders(experts)]
    held = [[] for _ in parts]
    for stage in range(len(orders[0])):
        for k, order in enumerate(orders):
            bit = order[stage]
            axis = sum(1 for other in held[k] if other > bit)
            parts[k] = jnp.stack([parts[k], swap(parts[k], bit, experts)], axis=axis)
            held[k].append(bit)
    rows = experts // 2 * block.shape[0]
    return jnp.concatenate([part.reshape(rows, part.shape[-1]) for part in parts], axis=1)


def scatter_chips(total, experts):
    orders = exchange_orders(experts)
    bits = len(orders[0])
    rows = total.shape[0] >> bits
    parts = [
        total[:, low:high].reshape((2,) * bits + (rows, high - low))
        for low, high in column_parts(total.shape[1])
    ]
    left = [sorted(order, reverse=True) for order in orders]
    for stage in range(bits):
        for k, order in enumerate(orders):
            bit = order[stage]
            axis = left[k].index(bit)
            kept = lax.index_in_dim(parts[k], 0, axis, keepdims=False)
            sent = lax.index_in_dim(parts[k], 1, axis, keepdims=False)
            came = swap(sent, bit, experts)
            parts[k] = (kept.astype(jnp.float32) + came.astype(jnp.float32)).astype(jnp.bfloat16)
            left[k].remove(bit)
    return jnp.concatenate(parts, axis=1)


def local(tokens, expert_ids, gate_weights, host, w_in, w_out):
    experts = lax.axis_size("expert")
    tok_dev, top_count = expert_ids.shape
    d_model = tokens.shape[1]
    slot_count = max(
        2, min(tok_dev // 2, (3 * tok_dev * top_count + 2 * experts - 1) // (2 * experts))
    )
    sources = experts // 2
    together = 4 if slot_count >= 16 else 8
    groups = sources // together
    group_rows = together * slot_count
    group_tokens = together * tok_dev
    total = groups * group_rows
    mine = host[lax.axis_index("expert")]
    sibling = [(device, device ^ 1) for device in range(experts)]

    high = lax.reduce_precision(gate_weights, 8, 7)
    middle = lax.reduce_precision(gate_weights - high, 8, 7)
    low = gate_weights - high - middle
    routing = jnp.concatenate([expert_ids.astype(jnp.float32), high, middle, low], axis=1)
    routing = jnp.pad(routing, ((0, 0), (0, 128 - 4 * top_count)))
    outgoing = jnp.concatenate([tokens, routing.astype(jnp.bfloat16)], axis=1)
    own = gather_chips(outgoing, experts)
    other = lax.ppermute(own, "expert", sibling)

    halves, _, _, half = w_in.shape[1:]
    first = w_in[0].reshape(halves, d_model, 2 * half)
    second = w_out[0].reshape(halves * half, d_model)

    def partial_rows(gathered):
        routing = gathered[:, d_model:].astype(jnp.float32)
        ids, high, middle, low = (
            routing[:, part * top_count:(part + 1) * top_count] for part in range(4)
        )
        hit = ids == mine.astype(jnp.float32)
        gate = jnp.sum(jnp.where(hit, high + middle + low, 0.0), axis=1).reshape(groups, group_tokens)
        named = jnp.any(hit, axis=1).reshape(sources, tok_dev)
        earlier = jnp.arange(tok_dev)[:, None] < jnp.arange(tok_dev)[None, :]
        rank = jnp.dot(
            named.astype(jnp.float32), earlier.astype(jnp.float32), preferred_element_type=jnp.float32
        ).astype(jnp.int32)
        source = jnp.arange(sources, dtype=jnp.int32)[:, None] % together
        place = jnp.where(named, source * slot_count + rank, -1).reshape(groups, group_tokens)
        whole = lambda shape: pl.BlockSpec(
            shape, lambda i: (0,) * len(shape), pipeline_mode=pl.Buffered(1)
        )
        return pl.pallas_call(
            functools.partial(ffn_kernel, groups, 1, group_rows, 256),
            grid=(2 * groups + 1,),
            out_shape=jax.ShapeDtypeStruct((sources * tok_dev, d_model), jnp.bfloat16),
            in_specs=[
                whole(place.shape),
                whole(gate.shape),
                pl.BlockSpec((group_tokens, d_model), lambda i: (jnp.minimum(i, groups - 1), 0)),
                whole(first.shape),
                whole(second.shape),
            ],
            out_specs=pl.BlockSpec(
                (group_tokens, d_model), lambda i: (jnp.maximum(i - groups - 1, 0), 0)
            ),
            scratch_shapes=[
                pltpu.VMEM((total, d_model), jnp.bfloat16),
                pltpu.VMEM((total, 1), jnp.float32),
                pltpu.VMEM((total, halves * half), jnp.bfloat16),
                pltpu.VMEM((total, d_model), jnp.bfloat16),
            ],
            compiler_params=pltpu.CompilerParams(vmem_limit_bytes=56 * 1024 * 1024),
            cost_estimate=pl.CostEstimate(
                flops=17 * 10**9, bytes_accessed=40 * 10**6, transcendentals=10**6
            ),
        )(place, gate, gathered, first, second)

    kept = partial_rows(own)
    handed = lax.ppermute(partial_rows(other), "expert", sibling)
    summed = (kept.astype(jnp.float32) + handed.astype(jnp.float32)).astype(jnp.bfloat16)
    return scatter_chips(summed, experts)


def solution(mesh):
    in_specs = (
        P("expert", None),
        P("expert", None),
        P("expert", None),
        P(),
        P("expert", None, None, None, None),
        P("expert", None, None, None),
    )
    out_specs = P("expert", None)
    return jax.shard_map(local, mesh=mesh, in_specs=in_specs, out_specs=out_specs, check_vma=False)
```
